256 devices in a mesh: row: 8 (over z_lo, core), col: 16 (over y, x), seq: 2 (over z_hi).
Axes of the slice: x: 4, y: 4, z: 8 (z_hi: 2, z_lo: 4; z = z_hi * 4 + z_lo), core: 2. Of those that a mesh axis runs over, the one named last changes fastest.
Arguments:
- alignment: bfloat16 [64, 1024, 256], P('seq', ('row', 'col')), may hold values from -6 to 6
- left_weight: bfloat16 [256, 32], replicated, may hold values from -0.375 to 0.375
- right_weight: bfloat16 [256, 32], replicated, may hold values from -0.375 to 0.375
- out_weight: bfloat16 [1024, 128], replicated, may hold values from -0.1875 to 0.1875
- out_bias: float32 [128], replicated, may hold values from -3 to 3
- cotangent: bfloat16 [1024, 1024, 128], P(('row', 'seq'), 'col'), may hold values from -6 to 6
Outputs:
- pair_update: bfloat16 [1024, 1024, 128], P(('row', 'seq'), 'col')
- alignment_grad: float32 [64, 1024, 256], P('seq', ('row', 'col'))
- left_weight_grad: float32 [256, 32], replicated
- right_weight_grad: float32 [256, 32], replicated
- out_weight_grad: float32 [1024, 128], replicated
The draws below stay inside these ranges and needn't reach their ends.
All inputs are finite; a program needn't handle non-finite values.
Results may differ from the reference program's by a relative error of at most 0.02.
Values may be sent and summed in bfloat16 or wider, within the bound.
No kernel may reach another device: no remote copies, remote signals or barrier semaphores. Data moves between devices by JAX's collectives and lax.ppermute only.
A program may use at most 64 MiB of HBM per device.

```python
import math
import jax
import jax.numpy as jnp
from jax import lax

CM = 256
CP = 32
CZ = 128
SEQS = 64
RESIDUES = 1024


def shard_levels(key, shape, pieces, smallest, high):
    loudness, own = 1.0, jax.random.fold_in(key, 6)
    for dim, shards_of in pieces:
        steps = jnp.exp(jax.random.uniform(jax.random.fold_in(own, dim), (shards_of,), jnp.float32, smallest / len(pieces), high / len(pieces)))
        loudness = loudness * jnp.repeat(steps, shape[dim] // shards_of).reshape([-1 if axis == dim else 1 for axis in range(len(shape))])
    return loudness


def centred(own_key, shape, width, most, pieces=(), held_as=jnp.bfloat16):
    result = width * jax.random.normal(own_key, shape, jnp.float32)
    if pieces:
        result = result * shard_levels(own_key, shape, pieces, -0.22, 0.18)
    return jnp.clip(result, -most, most).astype(held_as)


def setup_inputs(seed: int = 0) -> dict:
    key_list = jax.random.split(jax.random.key(seed), 7)
    alignment = centred(key_list[0], (SEQS, RESIDUES, CM), 1.0, 6.0, ((0, 2), (1, 128)))
    left_weight = centred(key_list[1], (CM, CP), CM ** -0.5, 0.375)
    right_weight = centred(key_list[2], (CM, CP), CM ** -0.5, 0.375)
    out_weight = centred(key_list[3], (CP * CP, CZ), (CP * CP) ** -0.5, 0.1875)
    out_bias = centred(key_list[4], (CZ,), 0.5, 3.0, (), jnp.float32)
    cotangent = centred(key_list[5], (RESIDUES, RESIDUES, CZ), 1.0, 6.0, ((0, 16), (1, 16)))
    return dict(alignment=alignment, left_weight=left_weight, right_weight=right_weight, out_weight=out_weight, out_bias=out_bias, cotangent=cotangent)


def reference(alignment, left_weight, right_weight, out_weight, out_bias, cotangent):
    values = alignment.astype(jnp.float32)
    center = values - lax.optimization_barrier(jnp.mean(values, axis=2, keepdims=True))
    invstd = lax.rsqrt(lax.optimization_barrier(jnp.mean(center * center, axis=2, keepdims=True)) + 1e-05)
    scaled = center * invstd
    normed = scaled.astype(jnp.bfloat16)
    flat_normed = normed.reshape(SEQS * RESIDUES, CM)
    left = jnp.dot(flat_normed, left_weight, preferred_element_type=jnp.float32).astype(jnp.bfloat16)
    right = jnp.dot(flat_normed, right_weight, preferred_element_type=jnp.float32).astype(jnp.bfloat16)
    left_full = left.reshape(SEQS, RESIDUES, CP).astype(jnp.float32)
    right_full = right.reshape(SEQS, RESIDUES, CP).astype(jnp.float32)
    block_rows = math.gcd(RESIDUES, 32)
    block_count = RESIDUES // block_rows
    inverse = 1.0 / SEQS

    def one_block(carry, index):
        wout_total, right_total = carry
        start = (index * block_rows).astype(jnp.int32)
        left_piece = lax.dynamic_slice_in_dim(left_full, start, block_rows, 1)
        cot_flat = lax.dynamic_slice_in_dim(cotangent, start, block_rows, 0).reshape(block_rows * RESIDUES, CZ)
        outer = jnp.einsum('sic,sjd->ijcd', left_piece, right_full) * inverse
        outer_flat = outer.astype(jnp.bfloat16).reshape(block_rows * RESIDUES, CP * CP)
        pair = (jnp.dot(outer_flat, out_weight, preferred_element_type=jnp.float32) + out_bias).astype(jnp.bfloat16)
        wout_total = wout_total + lax.dot_general(outer_flat, cot_flat, (((0,), (0,)), ((), ())), preferred_element_type=jnp.float32)
        outer_grad = (jnp.dot(cot_flat, out_weight.T, preferred_element_type=jnp.float32) * inverse).astype(jnp.bfloat16)
        outer_grad = lax.optimization_barrier(outer_grad)
        outer_grad = outer_grad.astype(jnp.float32).reshape(block_rows, RESIDUES, CP, CP)
        left_part = jnp.einsum('ijcd,sjd->sic', outer_grad, right_full)
        right_total = right_total + jnp.einsum('ijcd,sic->sjd', outer_grad, left_piece)
        return ((wout_total, right_total), (pair, left_part))
    init = (jnp.zeros((CP * CP, CZ), jnp.float32), jnp.zeros((SEQS, RESIDUES, CP), jnp.float32))
    (wout_total, right_total), (pairs, left_parts) = lax.scan(one_block, init, jnp.arange(block_count, dtype=jnp.int32))
    pair_update = pairs.reshape(RESIDUES, RESIDUES, CZ)
    left_grad = left_parts.transpose(1, 0, 2, 3).reshape(SEQS * RESIDUES, CP).astype(jnp.bfloat16)
    right_grad = right_total.reshape(SEQS * RESIDUES, CP).astype(jnp.bfloat16)
    left_weight_grad = lax.dot_general(flat_normed, left_grad, (((0,), (0,)), ((), ())), preferred_element_type=jnp.float32) / RESIDUES
    right_weight_grad = lax.dot_general(flat_normed, right_grad, (((0,), (0,)), ((), ())), preferred_element_type=jnp.float32) / RESIDUES
    normed_grad = jnp.dot(left_grad, left_weight.T, preferred_element_type=jnp.float32) + jnp.dot(right_grad, right_weight.T, preferred_element_type=jnp.float32)
    normed_grad = normed_grad.reshape(SEQS, RESIDUES, CM)
    mean_grad = lax.optimization_barrier(jnp.mean(normed_grad, axis=2, keepdims=True))
    mean_cross = lax.optimization_barrier(jnp.mean(normed_grad * scaled, axis=2, keepdims=True))
    alignment_grad = invstd * (normed_grad - mean_grad - scaled * mean_cross)
    return (pair_update, alignment_grad, left_weight_grad, right_weight_grad, wout_total / RESIDUES)
```

```python
import jax
import jax.numpy as jnp
from jax import lax
from jax.experimental import pallas as pl
from jax.experimental.pallas import tpu as pltpu
from jax.sharding import PartitionSpec as P

F32 = jnp.float32
BF16 = jnp.bfloat16
LANES = 128
CP = 32
SEQ_HALF = 32
EPS = 1e-05


def dot(a, b, dims):
    return lax.dot_general(a, b, ((dims[:1], dims[1:]), ((), ())), preferred_element_type=F32)


def params(mib):
    return pltpu.CompilerParams(vmem_limit_bytes=mib << 20)


def normalize(x_ref, rows_ref):
    rows = x_ref[...].astype(F32).reshape(256, 256)
    halves = []
    for h in range(2):
        rows_ref[h] = rows[:, h * 128 : h * 128 + 128]
        halves.append(
            jnp.concatenate([rows_ref[h, pl.ds(i, SEQ_HALF, stride=8), :] for i in range(8)], axis=0)
        )
    values = jnp.concatenate(halves, axis=1)
    center = values - jnp.mean(values, axis=1, keepdims=True)
    invstd = lax.rsqrt(jnp.mean(center * center, axis=1, keepdims=True) + EPS)
    return center * invstd, invstd


def project_kernel(x_ref, weights_ref, left_ref, right_ref, rows_ref, block_ref):
    scaled, _ = normalize(x_ref, rows_ref)
    both = dot(weights_ref[...], scaled.astype(BF16), (1, 1))
    left_ref[0:32, :] = both[0:32, 0:128].astype(BF16)
    left_ref[32:64, :] = both[0:32, 128:256].astype(BF16)
    for j in range(8):
        block_ref[j * 8 : j * 8 + 8, :] = jnp.concatenate(
            [both[32 + k * 8 : 40 + k * 8, j * 32 : j * 32 + 32] for k in range(4)], axis=1
        )
    right_ref[...] = jnp.concatenate(
        [block_ref[pl.ds(h, 8, stride=8), :] for h in range(8)], axis=0
    ).astype(BF16)


def pair_kernel(
    left_in, right_in, cot_ref, w_scaled_ref, w_turned_ref, bias_ref,
    pair_ref, left_out, right_out, wout_ref,
    gathered, spread, left_ref, left_t_ref, grad, outer, left_sum, right_sum, wout_sum, wout_rows,
):
    lane = lax.broadcasted_iota(jnp.int32, (64, LANES), 1)
    for b in range(8):
        for half in range(2):
            left_ref[b * 64 : b * 64 + 64, half * 128 : half * 128 + 128] = left_in[b * 2 + half]
    left_t_ref[...] = left_ref[...].astype(F32).T.astype(BF16)
    gathered[...] = right_in[...].astype(F32)
    for h in range(8):
        for half in range(2):
            tile = jnp.concatenate(
                [gathered[r * 2 + half, h * 8 : h * 8 + 8, :] for r in range(8)], axis=0
            )
            turned = [tile] + [pltpu.roll(tile, k * 32, 1) for k in range(1, 4)]
            for d in range(4):
                for i in range(4):
                    spread[
                        h, d * 256 + i * 64 : d * 256 + i * 64 + 64, half * 128 : half * 128 + 128
                    ] = jnp.where(lane // 32 == i, turned[(i - d) % 4], 0.0).astype(BF16)

    def outer_grad_step(i, carry):
        cot = cot_ref[pl.ds(i * 4, 4)].reshape(256, LANES)
        rows = pl.ds(pl.multiple_of(i * 32, 32), 32)
        for h in range(8):
            piece = dot(w_scaled_ref[h * 128 : h * 128 + 128, :], cot, (1, 1)).astype(BF16)
            for d in range(4):
                grad[h, rows, d * 256 : d * 256 + 256] = piece[d * 32 : d * 32 + 32]
        return carry

    lax.fori_loop(0, 16, outer_grad_step, 0)

    left_sum[...] = jnp.zeros_like(left_sum)
    low = lax.broadcasted_iota(jnp.int32, (32, LANES), 1) < 64

    def grads_step(h, carry):
        left_sum[...] += dot(grad[h], spread[h], (1, 0))
        for half in range(2):
            parts = []
            part = dot(left_t_ref[half * 128 : half * 128 + 128, :], grad[h], (1, 0))
            for d in range(4):
                lo = part[:, d * 256 : d * 256 + 128]
                hi = part[:, d * 256 + 128 : d * 256 + 256]
                parts.append(
                    jnp.where(low, lo[0:32], lo[32:64]) + jnp.where(low, hi[64:96], hi[96:128])
                )
            turned = jnp.concatenate(parts, axis=0).T
            total = turned[0:64] + turned[64:128]
            for r in range(8):
                right_sum[r * 2 + half, pl.ds(pl.multiple_of(h * 8, 8), 8), :] = total[
                    r * 8 : r * 8 + 8
                ]
        return carry

    lax.fori_loop(0, 8, grads_step, 0)
    right_out[...] = right_sum[...].astype(BF16)
    for b in range(8):
        for half in range(2):
            left_out[b * 2 + half] = left_sum[
                b * 64 : b * 64 + 64, half * 128 : half * 128 + 128
            ].astype(BF16)

    left_ref[...] = (left_ref[...].astype(F32) * (1.0 / 64.0)).astype(BF16)

    def outer_step(h, carry):
        for d in range(4):
            piece = dot(left_ref[...], spread[h, d * 256 : d * 256 + 256, :], (1, 1)).astype(BF16)
            outer[:, pl.ds(pl.multiple_of(h * 128 + d * 32, 32), 32), :] = piece.reshape(16, 32, 256)
        return carry

    lax.fori_loop(0, 8, outer_step, 0)
    wout_sum[...] = jnp.zeros_like(wout_sum)

    def pair_step(i, carry):
        cot = cot_ref[pl.ds(i * 4, 4)].reshape(256, LANES)
        tile = outer[i]
        turned = dot(w_turned_ref[...], tile, (1, 0))
        pair_ref[pl.ds(i * 4, 4)] = (
            (turned.T + bias_ref[...]).astype(BF16).reshape(4, 64, LANES)
        )
        wout_sum[...] += dot(tile, cot, (1, 0))
        return carry

    lax.fori_loop(0, 16, pair_step, 0)
    for d in range(32):
        wout_rows[pl.ds(d, 32, stride=32), :] = wout_sum[d * 32 : d * 32 + 32, :]
    wout_ref[...] = wout_rows[...].astype(BF16)


def finish_kernel(x_ref, weights_ref, left_ref, right_ref, align_ref, weight_ref, rows_ref, block_ref):
    scaled, invstd = normalize(x_ref, rows_ref)
    block_ref[...] = right_ref[...].astype(F32)
    rows = [block_ref[pl.ds(j, 8, stride=8), :] for j in range(8)]
    right = jnp.concatenate(
        [
            jnp.concatenate([rows[j][:, k * 32 : k * 32 + 32] for j in range(8)], axis=1)
            for k in range(4)
        ],
        axis=0,
    )
    left = jnp.concatenate([left_ref[0:32, :], left_ref[32:64, :]], axis=1).astype(F32)
    grads = jnp.concatenate([left, right], axis=0).astype(BF16)
    weight = dot(grads, scaled.astype(BF16), (1, 0))
    weight_ref[0:64, :] = weight[:, 0:128].astype(BF16)
    weight_ref[64:128, :] = weight[:, 128:256].astype(BF16)
    normed_grad = dot(grads, weights_ref[...], (0, 0))
    mean_grad = jnp.mean(normed_grad, axis=1, keepdims=True)
    mean_cross = jnp.mean(normed_grad * scaled, axis=1, keepdims=True)
    result = invstd * (normed_grad - mean_grad - scaled * mean_cross)
    for h in range(2):
        for i in range(8):
            rows_ref[h, pl.ds(i, SEQ_HALF, stride=8), :] = result[
                i * 32 : i * 32 + 32, h * 128 : h * 128 + 128
            ]
        align_ref[:, h * 128 : h * 128 + 128] = rows_ref[h]


def body(alignment, left_weight, right_weight, out_weight, out_bias, cotangent):
    rows_n, cols_n, seq_n = lax.axis_size("row"), lax.axis_size("col"), lax.axis_size("seq")
    tile = ("row", "seq")
    to_left = [
        (c * seq_n + s, ((c % 8) * 2 + s) * seq_n + c // 8) for c in range(cols_n) for s in range(seq_n)
    ]
    to_right = [
        (r * cols_n + c, (c % 8) * cols_n + 2 * r + c // 8) for r in range(rows_n) for c in range(cols_n)
    ]
    swap = lambda pairs: [(b, a) for a, b in pairs]

    weights = jnp.concatenate(
        [left_weight.T, right_weight.T.reshape(8, 4, 256).transpose(1, 0, 2).reshape(32, 256)], axis=0
    )
    w_rows = out_weight.reshape(CP, CP, LANES).transpose(1, 0, 2).reshape(CP * CP, LANES)
    w_scaled = (w_rows.astype(F32) * (1.0 / 64.0)).astype(BF16)
    w_turned = w_rows.T

    block = jax.ShapeDtypeStruct((64, LANES), BF16)
    left_block, right_block = pl.pallas_call(
        project_kernel,
        out_shape=(block, block),
        scratch_shapes=[pltpu.VMEM((2, 256, LANES), F32), pltpu.VMEM((64, LANES), F32)],
        compiler_params=params(16),
        name="project",
    )(alignment, weights)

    left_block = lax.ppermute(left_block, ("col", "seq"), to_left)
    right_block = lax.ppermute(right_block, ("row", "col"), to_right)

    def gather(value, axes):
        return lax.all_to_all(
            jnp.broadcast_to(value, (16,) + value.shape), axes, 0, 0, tiled=True
        )

    left_all = gather(left_block, "col")
    right_all = gather(right_block, tile)

    blocks = jax.ShapeDtypeStruct((16, 64, LANES), BF16)
    pair, left_part, right_part, wout_part = pl.pallas_call(
        pair_kernel,
        out_shape=(
            jax.ShapeDtypeStruct((64, 64, LANES), BF16),
            blocks,
            blocks,
            jax.ShapeDtypeStruct((1024, LANES), BF16),
        ),
        scratch_shapes=[
            pltpu.VMEM((16, 64, LANES), F32),
            pltpu.VMEM((8, 1024, 256), BF16),
            pltpu.VMEM((512, 256), BF16),
            pltpu.VMEM((256, 512), BF16),
            pltpu.VMEM((8, 512, 1024), BF16),
            pltpu.VMEM((16, 1024, 256), BF16),
            pltpu.VMEM((512, 256), F32),
            pltpu.VMEM((16, 64, LANES), F32),
            pltpu.VMEM((1024, LANES), F32),
            pltpu.VMEM((1024, LANES), F32),
        ],
        compiler_params=params(48),
        name="pair_tile",
    )(left_all, right_all, cotangent, w_scaled, w_turned, out_bias.reshape(1, LANES))

    def total(value):
        return jnp.sum(value.astype(F32), axis=0)

    first = lax.all_to_all(
        jnp.concatenate([right_part, wout_part.reshape(16, 64, LANES)], axis=1), tile, 0, 0, tiled=True
    )
    first = total(first).astype(BF16)
    second = lax.all_to_all(
        jnp.concatenate([left_part, first[64:].reshape(16, 4, LANES)], axis=1), "col", 0, 0, tiled=True
    )
    second = total(second).astype(BF16)
    wout_piece = second[64:]
    left_grad = lax.ppermute(second[:64], ("col", "seq"), swap(to_left))
    right_grad = lax.ppermute(first[:64], ("row", "col"), swap(to_right))

    align_grad, weight_part = pl.pallas_call(
        finish_kernel,
        out_shape=(
            jax.ShapeDtypeStruct((256, 256), F32),
            jax.ShapeDtypeStruct((128, LANES), BF16),
        ),
        scratch_shapes=[pltpu.VMEM((2, 256, LANES), F32), pltpu.VMEM((64, LANES), F32)],
        compiler_params=params(16),
        name="finish",
    )(alignment, weights, left_grad, right_grad)

    weight_piece = total(
        lax.all_to_all(weight_part.reshape(16, 8, LANES), tile, 0, 0, tiled=True)
    ).astype(BF16)
    third = gather(jnp.concatenate([weight_piece, wout_piece], axis=0), "col")
    weight_piece = total(third[:, :8]).astype(BF16)
    last = gather(
        jnp.concatenate([third[:, 8:].reshape(64, LANES), weight_piece], axis=0), tile
    ).astype(F32) * (1.0 / 1024.0)
    wout_grad = last[:, :64].reshape(1024, LANES)
    halves = last[:, 64:].reshape(2, 64, LANES)
    weight_grad = jnp.concatenate([halves[0], halves[1]], axis=1)
    left_weight_grad = weight_grad[:32].T
    right_weight_grad = weight_grad[32:].reshape(4, 8, 256).transpose(1, 0, 2).reshape(32, 256).T
    return (
        pair,
        align_grad.reshape(alignment.shape),
        left_weight_grad,
        right_weight_grad,
        wout_grad,
    )


def solution(mesh):
    placed = (P("seq", ("row", "col"), None), P(), P(), P(), P(), P(("row", "seq"), "col", None))
    return jax.shard_map(
        body,
        mesh=mesh,
        in_specs=placed,
        out_specs=(P(("row", "seq"), "col", None), P("seq", ("row", "col"), None), P(), P(), P()),
        check_vma=False,
    )
```

```python
import jax
import jax.numpy as jnp
from jax import lax
from jax.experimental import pallas as pl
from jax.experimental.pallas import tpu as pltpu
from jax.sharding import Mesh, PartitionSpec as P

F32 = jnp.float32
BF16 = jnp.bfloat16
LANES = 128
CP = 32
SEQ_HALF = 32
EPS = 1e-05


def dot(a, b, dims):
    return lax.dot_general(a, b, ((dims[:1], dims[1:]), ((), ())), preferred_element_type=F32)


def params(mib):
    return pltpu.CompilerParams(vmem_limit_bytes=mib << 20)


def normalize(x_ref, rows_ref):
    rows = x_ref[...].astype(F32).reshape(256, 256)
    halves = []
    for h in range(2):
        rows_ref[h] = rows[:, h * 128 : h * 128 + 128]
        halves.append(
            jnp.concatenate([rows_ref[h, pl.ds(i, SEQ_HALF, stride=8), :] for i in range(8)], axis=0)
        )
    values = jnp.concatenate(halves, axis=1)
    center = values - jnp.mean(values, axis=1, keepdims=True)
    invstd = lax.rsqrt(jnp.mean(center * center, axis=1, keepdims=True) + EPS)
    return center * invstd, invstd


def project_kernel(x_ref, left_w, right_w, left_ref, right_ref, normed_ref, rows_ref, block_ref):
    scaled, _ = normalize(x_ref, rows_ref)
    normed = scaled.astype(BF16)
    normed_ref[...] = normed
    left = dot(left_w[...], normed, (1, 1))
    left_ref[0:32, :] = left[:, 0:128].astype(BF16)
    left_ref[32:64, :] = left[:, 128:256].astype(BF16)
    right = dot(right_w[...], normed, (1, 1))
    for half in range(2):
        rows_ref[0, 0:32, :] = right[:, half * 128 : half * 128 + 128]
        rows = [rows_ref[0, pl.ds(k, 8, stride=4), :] for k in range(4)]
        for j in range(4):
            block_ref[half * 32 + j * 8 : half * 32 + j * 8 + 8, :] = jnp.concatenate(
                [rows[k][:, j * 32 : j * 32 + 32] for k in range(4)], axis=1
            )
    right_ref[...] = jnp.concatenate(
        [block_ref[pl.ds(h, 8, stride=8), :] for h in range(8)], axis=0
    ).astype(BF16)


def pair_kernel(
    place_ref, left_in, right_own, right_other, cot_ref, w_scaled_ref, w_turned_ref, bias_ref,
    pair_ref, left_out, keep_out, send_out,
    gathered, spread, left_ref, left_t_ref, grad, outer, left_sum, right_sum, wout_sum, wout_rows,
):
    core = place_ref[0]
    lane = lax.broadcasted_iota(jnp.int32, (64, LANES), 1)
    low = lax.broadcasted_iota(jnp.int32, (32, LANES), 1) < 64
    for b in range(8):
        for half in range(2):
            left_ref[b * 64 : b * 64 + 64, half * 128 : half * 128 + 128] = left_in[half * 8 + b]
    left_t_ref[...] = left_ref[...].astype(F32).T.astype(BF16)
    for z in range(4):
        for half in range(2):
            gathered[(z * 2 + core) * 2 + half] = right_own[z * 2 + half].astype(F32)
            gathered[(z * 2 + 1 - core) * 2 + half] = right_other[z * 2 + half].astype(F32)
    for h in range(8):
        for half in range(2):
            tile = jnp.concatenate(
                [gathered[r * 2 + half, h * 8 : h * 8 + 8, :] for r in range(8)], axis=0
            )
            turned = [tile] + [pltpu.roll(tile, k * 32, 1) for k in range(1, 4)]
            for d in range(4):
                for i in range(4):
                    spread[
                        h, d * 256 + i * 64 : d * 256 + i * 64 + 64, half * 128 : half * 128 + 128
                    ] = jnp.where(lane // 32 == i, turned[(i - d) % 4], 0.0).astype(BF16)

    for i in range(16):
        cot = cot_ref[i * 4 : i * 4 + 4].reshape(256, LANES)
        for h in range(8):
            piece = dot(w_scaled_ref[h * 128 : h * 128 + 128, :], cot, (1, 1)).astype(BF16)
            for d in range(4):
                grad[h, i * 32 : i * 32 + 32, d * 256 : d * 256 + 256] = piece[d * 32 : d * 32 + 32]

    for h in range(8):
        part = dot(grad[h], spread[h], (1, 0))
        left_sum[...] = part if h == 0 else left_sum[...] + part
        for half in range(2):
            parts = []
            part = dot(left_t_ref[half * 128 : half * 128 + 128, :], grad[h], (1, 0))
            for d in range(4):
                lo = part[:, d * 256 : d * 256 + 128]
                hi = part[:, d * 256 + 128 : d * 256 + 256]
                parts.append(
                    jnp.where(low, lo[0:32], lo[32:64]) + jnp.where(low, hi[64:96], hi[96:128])
                )
            turned = jnp.concatenate(parts, axis=0).T
            total = turned[0:64] + turned[64:128]
            for r in range(8):
                right_sum[r * 2 + half, h * 8 : h * 8 + 8, :] = total[r * 8 : r * 8 + 8]
    for b in range(8):
        for half in range(2):
            left_out[half * 8 + b] = left_sum[
                b * 64 : b * 64 + 64, half * 128 : half * 128 + 128
            ].astype(BF16)

    left_ref[...] = (left_ref[...].astype(F32) * (1.0 / 64.0)).astype(BF16)
    for h in range(8):
        for d in range(4):
            piece = dot(left_ref[...], spread[h, d * 256 : d * 256 + 256, :], (1, 1)).astype(BF16)
            first = h * 128 + d * 32
            outer[:, first : first + 32, :] = piece.reshape(16, 32, 256)

    for i in range(16):
        cot = cot_ref[i * 4 : i * 4 + 4].reshape(256, LANES)
        tile = outer[i]
        turned = dot(w_turned_ref[...], tile, (1, 0))
        pair_ref[i * 4 : i * 4 + 4] = (
            (turned.T + bias_ref[...]).astype(BF16).reshape(4, 64, LANES)
        )
        part = dot(tile, cot, (1, 0))
        wout_sum[...] = part if i == 0 else wout_sum[...] + part
    for t in range(16):
        for q in range(4):
            wout_rows[pl.ds(t * 64 + q, 16, stride=4), :] = wout_sum[
                pl.ds(((t % 8) * 4 + q) * 32 + t // 8, 16, stride=2), :
            ]
    for z in range(4):
        for half in range(2):
            for out, owner in ((keep_out, core), (send_out, 1 - core)):
                b = (z * 2 + owner) * 2 + half
                out[z * 2 + half, 0:64] = right_sum[b].astype(out.dtype)
                out[z * 2 + half, 64:128] = wout_rows[
                    pl.ds(pl.multiple_of(b * 64, 64), 64), :
                ].astype(out.dtype)


def turn_grads(left, right, rows_ref, turn_ref):
    rows_ref[...] = right
    rows = [rows_ref[pl.ds(j, 8, stride=8), :] for j in range(8)]
    for half in range(2):
        for k in range(4):
            turn_ref[half, pl.ds(k, 8, stride=4), :] = jnp.concatenate(
                [rows[half * 4 + j][:, k * 32 : k * 32 + 32] for j in range(4)], axis=1
            )
    right = jnp.concatenate([turn_ref[0], turn_ref[1]], axis=1).astype(BF16)
    left = jnp.concatenate([left[0:32], left[32:64]], axis=1).astype(BF16)
    return left, right


def weights_kernel(left_ref, right_ref, wout_ref, normed_ref, next_ref, rows_ref, turn_ref):
    left, right = turn_grads(
        left_ref[...].astype(F32), right_ref[...].astype(F32), rows_ref, turn_ref
    )
    wout = wout_ref[...].astype(F32)
    total = dot(jnp.concatenate([left, right], axis=0), normed_ref[...], (1, 0)).astype(BF16)
    for half in range(2):
        for b in range(8):
            next_ref[half * 8 + b, 0:8, :] = total[b * 8 : b * 8 + 8, half * 128 : half * 128 + 128]
    for b in range(16):
        next_ref[b, 8:12, :] = wout[b * 4 : b * 4 + 4].astype(BF16)
    next_ref[:, 12:16, :] = jnp.zeros((16, 4, LANES), BF16)


def align_kernel(x_ref, left_w, right_w, left_ref, right_ref, align_ref, rows_ref, block_ref, turn_ref):
    scaled, invstd = normalize(x_ref, rows_ref)
    left, right = turn_grads(
        left_ref[...].astype(F32), right_ref[...].astype(F32), block_ref, turn_ref
    )
    normed_grad = dot(left, left_w[...], (0, 0)) + dot(right, right_w[...], (0, 0))
    mean_grad = jnp.mean(normed_grad, axis=1, keepdims=True)
    mean_cross = jnp.mean(normed_grad * scaled, axis=1, keepdims=True)
    result = invstd * (normed_grad - mean_grad - scaled * mean_cross)
    for h in range(2):
        for i in range(8):
            rows_ref[h, pl.ds(i, SEQ_HALF, stride=8), :] = result[
                i * 32 : i * 32 + 32, h * 128 : h * 128 + 128
            ]
        align_ref[:, h * 128 : h * 128 + 128] = rows_ref[h]


def last_kernel(in_ref, wout_ref, left_ref, right_ref):
    for b in range(16):
        wout_ref[b * 64 : b * 64 + 64, :] = in_ref[b, 0:64].astype(F32) * (1.0 / 1024.0)
    for half in range(2):
        for out, first in ((left_ref, 0), (right_ref, 4)):
            for b in range(4):
                out[b * 8 : b * 8 + 8, half * 128 : half * 128 + 128] = in_ref[
                    half * 8 + first + b, 64:72
                ].astype(F32) * (1.0 / 1024.0)


def body(alignment, left_weight, right_weight, out_weight, out_bias, cotangent):
    rows_n, cols_n, seq_n = 8, lax.axis_size("col"), lax.axis_size("seq")
    row, column = ("z", "core"), ("z", "seq")
    to_left = [
        (c * seq_n + s, c * seq_n + s if c // 8 == s else (c ^ 8) * seq_n + 1 - s)
        for c in range(cols_n)
        for s in range(seq_n)
    ]
    to_right = [
        (r * cols_n + c, (c % 8) * cols_n + 2 * r + c // 8) for r in range(rows_n) for c in range(cols_n)
    ]
    back = [(b, a) for a, b in to_right]
    struct = jax.ShapeDtypeStruct
    vmem = pltpu.VMEM
    left_w, right_w = left_weight.T, right_weight.T
    w_rows = out_weight.reshape(CP, CP, LANES).transpose(1, 0, 2).reshape(CP * CP, LANES)
    w_scaled = (w_rows.astype(F32) * (1.0 / 64.0)).astype(BF16)
    w_turned = w_rows.T
    place = jnp.stack([lax.axis_index("core"), lax.axis_index("seq")]).astype(jnp.int32)
    smem = pl.BlockSpec(memory_space=pltpu.SMEM)

    def exchange(value, axes):
        return lax.all_to_all(value, axes, 0, 0, tiled=True)

    def gather(value, axes, count):
        return exchange(jnp.broadcast_to(value, (count,) + value.shape), axes)

    def total(value):
        return jnp.sum(value.astype(F32), axis=0).astype(BF16)

    def other_core(value):
        return lax.ppermute(value, "core", [(0, 1), (1, 0)])

    def cost(flops, nbytes):
        return pl.CostEstimate(flops=flops, bytes_accessed=nbytes, transcendentals=0)

    def in_hbm(value):
        return pltpu.with_memory_space_constraint(value, pltpu.HBM)

    block = struct((64, LANES), BF16)
    left_block, right_block, normed = pl.pallas_call(
        project_kernel,
        out_shape=(block, block, struct((256, 256), BF16)),
        scratch_shapes=[vmem((2, 256, LANES), F32), vmem((64, LANES), F32)],
        compiler_params=params(8),
        name="project",
    )(in_hbm(alignment), in_hbm(left_w), in_hbm(right_w))

    right_block = lax.ppermute(right_block, row + ("col",), to_right)
    left_block = lax.ppermute(left_block, ("col", "seq"), to_left)
    right_own = gather(right_block, column, 8)
    left_all = gather(left_block, "col", 16)
    right_other = other_core(right_own)

    vm = pl.BlockSpec(memory_space=vmem)
    pair, left_part, keep, send = pl.pallas_call(
        pair_kernel,
        in_specs=[smem] + [vm] * 7,
        out_shape=(
            struct((64, 64, LANES), BF16),
            struct((16, 64, LANES), BF16),
            struct((8, 128, LANES), F32),
            struct((8, 128, LANES), BF16),
        ),
        scratch_shapes=[
            vmem((16, 64, LANES), F32),
            vmem((8, 1024, 256), BF16),
            vmem((512, 256), BF16),
            vmem((256, 512), BF16),
            vmem((8, 512, 1024), BF16),
            vmem((16, 1024, 256), BF16),
            vmem((512, 256), F32),
            vmem((16, 64, LANES), F32),
            vmem((1024, LANES), F32),
            vmem((1024, LANES), F32),
        ],
        compiler_params=params(40),
        cost_estimate=cost(8 << 30, 6 << 20),
        name="pair_tile",
    )(
        place,
        left_all,
        right_own,
        right_other,
        cotangent,
        w_scaled,
        w_turned,
        out_bias.reshape(1, LANES),
    )

    left_back = exchange(left_part, "col")
    right_send = (keep + other_core(send).astype(F32)).astype(BF16)
    right_send, left_back = lax.optimization_barrier((right_send, left_back))
    left_grad = lax.ppermute(total(left_back), ("col", "seq"), to_left)
    first = total(exchange(right_send, column))
    right_grad = lax.ppermute(first[:64], row + ("col",), back)
    stage = pl.pallas_call(
        weights_kernel,
        out_shape=struct((16, 16, LANES), BF16),
        scratch_shapes=[vmem((64, LANES), F32), vmem((2, 32, LANES), F32)],
        compiler_params=params(8),
        name="weight_grads",
    )(left_grad, right_grad, first[64:], normed)

    stage = gather(total(exchange(stage, "col")), ("z", "core", "seq"), 16)
    last = gather(
        jnp.concatenate(
            [stage[:, 8:12].reshape(64, LANES), total(stage[:, :8]), jnp.zeros((8, LANES), BF16)], axis=0
        ),
        "col",
        16,
    )
    align_grad = pl.pallas_call(
        align_kernel,
        out_shape=struct((256, 256), F32),
        scratch_shapes=[vmem((2, 256, LANES), F32), vmem((64, LANES), F32), vmem((2, 32, LANES), F32)],
        compiler_params=params(8),
        cost_estimate=cost(1 << 24, 1 << 20),
        name="align",
    )(in_hbm(alignment), left_w, right_w, left_grad, right_grad)
    wout_grad, left_weight_grad, right_weight_grad = pl.pallas_call(
        last_kernel,
        out_shape=(struct((1024, LANES), F32), struct((32, 256), F32), struct((32, 256), F32)),
        compiler_params=params(8),
        name="last",
    )(last)
    return (
        pair,
        align_grad.reshape(alignment.shape),
        left_weight_grad.T,
        right_weight_grad.T,
        wout_grad,
    )


def solution(mesh):
    z = mesh.shape["row"] // 2
    fine = Mesh(
        mesh.devices.reshape(z, 2, mesh.shape["col"], mesh.shape["seq"]), ("z", "core", "col", "seq")
    )
    row = ("z", "core")
    tiles, blocks = P(row + ("seq",), "col", None), P("seq", row + ("col",), None)
    return jax.shard_map(
        body,
        mesh=fine,
        in_specs=(blocks, P(), P(), P(), P(), tiles),
        out_specs=(tiles, blocks, P(), P(), P()),
        check_vma=False,
    )
```

```python
import jax
import jax.numpy as jnp
from jax import lax
from jax.experimental import pallas as pl
from jax.experimental.pallas import tpu as pltpu
from jax.sharding import Mesh, PartitionSpec as P

F32 = jnp.float32
BF16 = jnp.bfloat16
LANES = 128
CP = 32
SEQ_HALF = 32
EPS = 1e-05


def dot(a, b, dims):
    return lax.dot_general(a, b, ((dims[:1], dims[1:]), ((), ())), preferred_element_type=F32)


def params(mib):
    return pltpu.CompilerParams(vmem_limit_bytes=mib << 20)


def normalize(x_ref, rows_ref):
    rows = x_ref[...].astype(F32).reshape(256, 256)
    halves = []
    for h in range(2):
        rows_ref[h] = rows[:, h * 128 : h * 128 + 128]
        halves.append(
            jnp.concatenate([rows_ref[h, pl.ds(i, SEQ_HALF, stride=8), :] for i in range(8)], axis=0)
        )
    values = jnp.concatenate(halves, axis=1)
    center = values - jnp.mean(values, axis=1, keepdims=True)
    invstd = lax.rsqrt(jnp.mean(center * center, axis=1, keepdims=True) + EPS)
    return center * invstd, invstd


def project_kernel(x_ref, left_w, right_w, both_ref, normed_ref, rows_ref, block_ref):
    scaled, _ = normalize(x_ref, rows_ref)
    normed = scaled.astype(BF16)
    normed_ref[...] = normed
    left = dot(left_w[...], normed, (1, 1))
    left = jnp.concatenate([left[:, 0:128], left[:, 128:256]], axis=0).astype(BF16)
    right = dot(right_w[...], normed, (1, 1))
    for half in range(2):
        rows_ref[0, 0:32, :] = right[:, half * 128 : half * 128 + 128]
        rows = [rows_ref[0, pl.ds(k, 8, stride=4), :] for k in range(4)]
        for j in range(4):
            block_ref[half * 32 + j * 8 : half * 32 + j * 8 + 8, :] = jnp.concatenate(
                [rows[k][:, j * 32 : j * 32 + 32] for k in range(4)], axis=1
            )
    right = jnp.concatenate(
        [block_ref[pl.ds(h, 8, stride=8), :] for h in range(8)], axis=0
    ).astype(BF16)
    for b in range(8):
        both_ref[b, 0:64] = right
        both_ref[b, 64:128] = left


def route_kernel(own_ref, other_ref, out_ref):
    core, upper, z_own = lax.axis_index("core"), lax.axis_index("col") // 8, lax.axis_index("z")
    left = [own_ref[z_own * 2 + half, 64:128] for half in range(2)]
    none = jnp.zeros((LANES, LANES), BF16)
    for c in range(16):
        out_ref[c, 0:64] = left[0]
        out_ref[c, 64:128] = left[1]
    for z in range(4):
        for owner, rights in ((core, own_ref), (1 - core, other_ref)):
            c = (z * 2 + owner) * 2
            out_ref[c + upper, 128:192] = rights[z * 2, 0:64]
            out_ref[c + upper, 192:256] = rights[z * 2 + 1, 0:64]
            out_ref[c + 1 - upper, 128:256] = none


def fill(blocks, left_ref, gathered, spread):
    odd, seq = lax.axis_index("col") % 2, lax.axis_index("seq")
    lane = lax.broadcasted_iota(jnp.int32, (64, LANES), 1)
    for b in range(8):
        for half in range(2):
            left_ref[b * 64 : b * 64 + 64, half * 128 : half * 128 + 128] = blocks[
                seq * 8 + b, half * 64 : half * 64 + 64
            ]
            gathered[b * 2 + half] = blocks[
                odd * 8 + b, 128 + half * 64 : 192 + half * 64
            ].astype(F32)
    for h in range(8):
        for half in range(2):
            tile = jnp.concatenate(
                [gathered[r * 2 + half, h * 8 : h * 8 + 8, :] for r in range(8)], axis=0
            )
            turned = [tile] + [pltpu.roll(tile, k * 32, 1) for k in range(1, 4)]
            for d in range(4):
                for i in range(4):
                    spread[
                        h, d * 256 + i * 64 : d * 256 + i * 64 + 64, half * 128 : half * 128 + 128
                    ] = jnp.where(lane // 32 == i, turned[(i - d) % 4], 0.0).astype(BF16)


def grads_kernel(
    blocks, cot_hbm, w_scaled_ref, out_ref,
    cot_ref, gathered, spread, left_ref, left_t_ref, grad, left_sum, right_sum, arrived,
):
    copy = pltpu.make_async_copy(cot_hbm, cot_ref, arrived)
    copy.start()
    odd, seq = lax.axis_index("col") % 2, lax.axis_index("seq")
    low = lax.broadcasted_iota(jnp.int32, (32, LANES), 1) < 64
    fill(blocks, left_ref, gathered, spread)
    left_t_ref[...] = left_ref[...].astype(F32).T.astype(BF16)
    copy.wait()
    for i in range(16):
        cot = cot_ref[i * 4 : i * 4 + 4].reshape(256, LANES)
        for h in range(8):
            piece = dot(w_scaled_ref[h * 128 : h * 128 + 128, :], cot, (1, 1)).astype(BF16)
            for d in range(4):
                grad[h, i * 32 : i * 32 + 32, d * 256 : d * 256 + 256] = piece[d * 32 : d * 32 + 32]
    for h in range(8):
        part = dot(grad[h], spread[h], (1, 0))
        left_sum[...] = part if h == 0 else left_sum[...] + part
        for half in range(2):
            parts = []
            part = dot(left_t_ref[half * 128 : half * 128 + 128, :], grad[h], (1, 0))
            for d in range(4):
                lo = part[:, d * 256 : d * 256 + 128]
                hi = part[:, d * 256 + 128 : d * 256 + 256]
                parts.append(
                    jnp.where(low, lo[0:32], lo[32:64]) + jnp.where(low, hi[64:96], hi[96:128])
                )
            turned = jnp.concatenate(parts, axis=0).T
            total = turned[0:64] + turned[64:128]
            for r in range(8):
                right_sum[r * 2 + half, h * 8 : h * 8 + 8, :] = total[r * 8 : r * 8 + 8]
    none = jnp.zeros((LANES, LANES), BF16)
    for b in range(8):
        for half in range(2):
            out_ref[seq * 8 + b, half * 64 : half * 64 + 64] = left_sum[
                b * 64 : b * 64 + 64, half * 128 : half * 128 + 128
            ].astype(BF16)
            out_ref[odd * 8 + b, 128 + half * 64 : 192 + half * 64] = right_sum[
                b * 2 + half
            ].astype(BF16)
        out_ref[(1 - seq) * 8 + b, 0:128] = none
        out_ref[(1 - odd) * 8 + b, 128:256] = none


def pair_kernel(
    blocks, cot_ref, w_turned_ref, bias_ref, pair_ref, keep_out, send_out,
    gathered, spread, left_ref, outer, wout_sum, wout_rows,
):
    core = lax.axis_index("core")
    fill(blocks, left_ref, gathered, spread)
    left_ref[...] = (left_ref[...].astype(F32) * (1.0 / 64.0)).astype(BF16)
    for h in range(8):
        for d in range(4):
            piece = dot(left_ref[...], spread[h, d * 256 : d * 256 + 256, :], (1, 1)).astype(BF16)
            first = h * 128 + d * 32
            outer[:, first : first + 32, :] = piece.reshape(16, 32, 256)
    for i in range(16):
        cot = cot_ref[i * 4 : i * 4 + 4].reshape(256, LANES)
        tile = outer[i]
        turned = dot(w_turned_ref[...], tile, (1, 0))
        pair_ref[i * 4 : i * 4 + 4] = (
            (turned.T + bias_ref[...]).astype(BF16).reshape(4, 64, LANES)
        )
        part = dot(tile, cot, (1, 0))
        wout_sum[...] = part if i == 0 else wout_sum[...] + part
    for d in range(32):
        wout_rows[pl.ds(d, 32, stride=32), :] = wout_sum[d * 32 : d * 32 + 32, :]
    for z in range(4):
        for half in range(2):
            for out, owner in ((keep_out, core), (send_out, 1 - core)):
                b = (z * 2 + owner) * 2 + half
                out[z * 2 + half] = wout_rows[pl.ds(pl.multiple_of(b * 64, 64), 64), :].astype(BF16)


def sort_kernel(back_ref, keep_w, send_w, left_ref, other_ref, keep_ref, send_ref):
    core, upper, seq = lax.axis_index("core"), lax.axis_index("col") // 8, lax.axis_index("seq")
    for half, out in ((seq, left_ref), (1 - seq, other_ref)):
        rows = pl.ds(pl.multiple_of(half * 64, 64), 64)
        left = back_ref[0, rows].astype(F32)
        for b in range(1, 16):
            left += back_ref[b, rows].astype(F32)
        out[...] = left.astype(BF16)
    for z in range(4):
        for half in range(2):
            for out, owner, wout in ((keep_ref, core, keep_w), (send_ref, 1 - core, send_w)):
                c = (z * 2 + owner) * 2 + upper
                out[z * 2 + half, 0:64] = back_ref[c, 128 + half * 64 : 192 + half * 64]
                out[z * 2 + half, 64:128] = wout[z * 2 + half]


def turn_grads(left, right, rows_ref, turn_ref):
    rows_ref[...] = right
    rows = [rows_ref[pl.ds(j, 8, stride=8), :] for j in range(8)]
    for half in range(2):
        for k in range(4):
            turn_ref[half, pl.ds(k, 8, stride=4), :] = jnp.concatenate(
                [rows[half * 4 + j][:, k * 32 : k * 32 + 32] for j in range(4)], axis=1
            )
    right = jnp.concatenate([turn_ref[0], turn_ref[1]], axis=1).astype(BF16)
    left = jnp.concatenate([left[0:32], left[32:64]], axis=1).astype(BF16)
    return left, right


def weights_kernel(
    left_ref, partner_ref, right_ref, normed_ref, partner_normed, keep_ref, send_ref, rows_ref, turn_ref, total_ref
):
    core = lax.axis_index("core")
    left, right = turn_grads(
        left_ref[...].astype(F32), right_ref[...].astype(F32), rows_ref, turn_ref
    )
    partner = jnp.concatenate([partner_ref[0:32], partner_ref[32:64]], axis=1)
    left = dot(left, normed_ref[...], (1, 0)) + dot(partner, partner_normed[...], (1, 0))
    total = jnp.concatenate([left, dot(right, normed_ref[...], (1, 0))], axis=0)
    total_ref[0] = total[:, 0:128]
    total_ref[1] = total[:, 128:256]
    keep_ref[...] = total_ref[core]
    send_ref[...] = total_ref[1 - core].astype(BF16)


def align_kernel(x_ref, left_w, right_w, left_ref, right_ref, align_ref, rows_ref, block_ref, turn_ref):
    scaled, invstd = normalize(x_ref, rows_ref)
    left, right = turn_grads(
        left_ref[...].astype(F32), right_ref[...].astype(F32), block_ref, turn_ref
    )
    normed_grad = dot(left, left_w[...], (0, 0)) + dot(right, right_w[...], (0, 0))
    mean_grad = jnp.mean(normed_grad, axis=1, keepdims=True)
    mean_cross = jnp.mean(normed_grad * scaled, axis=1, keepdims=True)
    result = invstd * (normed_grad - mean_grad - scaled * mean_cross)
    for h in range(2):
        for i in range(8):
            rows_ref[h, pl.ds(i, SEQ_HALF, stride=8), :] = result[
                i * 32 : i * 32 + 32, h * 128 : h * 128 + 128
            ]
        align_ref[:, h * 128 : h * 128 + 128] = rows_ref[h]


def last_kernel(own_ref, other_ref, wout_ref, left_ref, right_ref):
    core = lax.axis_index("core")
    sums = []
    for blocks in (own_ref, other_ref):
        weight = blocks[0, 0:64].astype(F32)
        for b in range(1, 8):
            weight += blocks[b, 0:64].astype(F32)
        sums.append(weight * (1.0 / 1024.0))
    for half, weight in enumerate(
        (jnp.where(core == 0, sums[0], sums[1]), jnp.where(core == 0, sums[1], sums[0]))
    ):
        left_ref[:, half * 128 : half * 128 + 128] = weight[0:32]
        right_ref[:, half * 128 : half * 128 + 128] = weight[32:64]
    for z in range(4):
        for half in range(2):
            for blocks, owner in ((own_ref, core), (other_ref, 1 - core)):
                start = pl.multiple_of(((z * 2 + owner) * 2 + half) * 64, 64)
                wout_ref[pl.ds(start, 64), :] = blocks[z * 2 + half, 64:128].astype(F32) * (
                    1.0 / 1024.0
                )


def body(alignment, left_weight, right_weight, out_weight, out_bias, cotangent):
    cols_n, seq_n = lax.axis_size("col"), lax.axis_size("seq")
    column = ("z", "seq")
    to_partner = [(c * seq_n + c // 8, c * seq_n + 1 - c // 8) for c in range(cols_n)]
    struct = jax.ShapeDtypeStruct
    vmem = pltpu.VMEM
    left_w, right_w = left_weight.T, right_weight.T
    w_rows = out_weight.reshape(CP, CP, LANES).transpose(1, 0, 2).reshape(CP * CP, LANES)
    w_scaled = (w_rows.astype(F32) * (1.0 / 64.0)).astype(BF16)
    w_turned = w_rows.T
    col = lax.axis_index("col")
    seq = lax.axis_index("seq")
    def exchange(value, axes):
        return lax.all_to_all(value, axes, 0, 0, tiled=True)

    def gather(value, axes, count):
        return exchange(jnp.broadcast_to(value, (count,) + value.shape), axes)

    def total(value):
        return jnp.sum(value.astype(F32), axis=0).astype(BF16)

    def other_core(value):
        return lax.ppermute(value, "core", [(0, 1), (1, 0)])

    def cost(flops, nbytes):
        return pl.CostEstimate(flops=flops, bytes_accessed=nbytes, transcendentals=0)

    def in_hbm(value):
        return pltpu.with_memory_space_constraint(value, pltpu.HBM)

    block = struct((64, LANES), BF16)
    both, normed = pl.pallas_call(
        project_kernel,
        out_shape=(struct((8, 128, LANES), BF16), struct((256, 256), BF16)),
        scratch_shapes=[vmem((2, 256, LANES), F32), vmem((64, LANES), F32)],
        compiler_params=params(8),
        name="project",
    )(in_hbm(alignment), in_hbm(left_w), in_hbm(right_w))

    both = exchange(both, column)
    vm, hbm = pl.BlockSpec(memory_space=vmem), pl.BlockSpec(memory_space=pl.ANY)
    blocks = pl.pallas_call(
        route_kernel,
        in_specs=[vm, vm],
        out_shape=struct((16, 256, LANES), BF16),
        compiler_params=params(8),
        name="route",
    )(both, other_core(both))
    blocks = exchange(blocks, "col")
    partner_normed = lax.ppermute(normed, ("col", "seq"), [(b, a) for a, b in to_partner])
    blocks, partner_normed = lax.optimization_barrier((blocks, partner_normed))

    gathered, spread = vmem((16, 64, LANES), F32), vmem((8, 1024, 256), BF16)
    left_rows = vmem((512, 256), BF16)
    back = pl.pallas_call(
        grads_kernel,
        in_specs=[vm, hbm, vm],
        out_shape=struct((16, 256, LANES), BF16),
        scratch_shapes=[
            vmem((64, 64, LANES), BF16),
            gathered,
            spread,
            left_rows,
            vmem((256, 512), BF16),
            vmem((8, 512, 1024), BF16),
            vmem((512, 256), F32),
            vmem((16, 64, LANES), F32),
            pltpu.SemaphoreType.DMA,
        ],
        compiler_params=params(24),
        cost_estimate=cost(4 << 30, 4 << 20),
        name="grads",
    )(blocks, in_hbm(cotangent), w_scaled)
    back = exchange(back, "col")
    eight = struct((8, 64, LANES), BF16)
    pair, keep, send = pl.pallas_call(
        pair_kernel,
        in_specs=[vm] * 4,
        out_shape=(struct((64, 64, LANES), BF16), eight, eight),
        scratch_shapes=[
            gathered,
            spread,
            left_rows,
            vmem((16, 1024, 256), BF16),
            vmem((1024, LANES), F32),
            vmem((1024, LANES), F32),
        ],
        compiler_params=params(24),
        cost_estimate=cost(4 << 30, 4 << 20),
        name="pair_tile",
    )(blocks, in_hbm(cotangent), w_turned, out_bias.reshape(1, LANES))
    sixteen = struct((8, 128, LANES), BF16)
    left_grad, other_left, keep, send = pl.pallas_call(
        sort_kernel,
        in_specs=[vm] * 3,
        out_shape=(block, block, sixteen, sixteen),
        compiler_params=params(8),
        name="sort",
    )(back, keep, send)
    first = total(exchange((keep.astype(F32) + other_core(send).astype(F32)).astype(BF16), column))
    right_grad = first[:64]
    keep_w, send_w = pl.pallas_call(
        weights_kernel,
        out_shape=(struct((64, LANES), F32), block),
        scratch_shapes=[
            vmem((64, LANES), F32),
            vmem((2, 32, LANES), F32),
            vmem((2, 64, LANES), F32),
        ],
        compiler_params=params(8),
        name="weight_grads",
    )(left_grad, other_left, right_grad, normed, partner_normed)
    weight = (keep_w + other_core(send_w).astype(F32)).astype(BF16)
    stage = total(gather(jnp.concatenate([weight, first[64:]], axis=0), "col", 16))
    other_left = lax.ppermute(other_left, ("col", "seq"), to_partner)
    stage, other_left = lax.optimization_barrier((stage, other_left))
    last = gather(stage, column, 8)
    home = lax.axis_index("col") // 8 == lax.axis_index("seq")
    left_grad = jnp.where(home, left_grad, other_left)
    align_grad = pl.pallas_call(
        align_kernel,
        out_shape=struct((256, 256), F32),
        scratch_shapes=[vmem((2, 256, LANES), F32), vmem((64, LANES), F32), vmem((2, 32, LANES), F32)],
        compiler_params=params(8),
        cost_estimate=cost(1 << 24, 1 << 20),
        name="align",
    )(in_hbm(alignment), left_w, right_w, left_grad, right_grad)
    last, align_grad = lax.optimization_barrier((last, align_grad))
    wout_grad, left_weight_grad, right_weight_grad = pl.pallas_call(
        last_kernel,
        out_shape=(struct((1024, LANES), F32), struct((32, 256), F32), struct((32, 256), F32)),
        compiler_params=params(8),
        name="last",
    )(last, other_core(last))
    return (
        pair,
        align_grad.reshape(alignment.shape),
        left_weight_grad.T,
        right_weight_grad.T,
        wout_grad,
    )


def solution(mesh):
    z = mesh.shape["row"] // 2
    fine = Mesh(
        mesh.devices.reshape(z, 2, mesh.shape["col"], mesh.shape["seq"]), ("z", "core", "col", "seq")
    )
    row = ("z", "core")
    tiles, blocks = P(row + ("seq",), "col", None), P("seq", row + ("col",), None)
    return jax.shard_map(
        body,
        mesh=fine,
        in_specs=(blocks, P(), P(), P(), P(), tiles),
        out_specs=(tiles, blocks, P(), P(), P()),
        check_vma=False,
    )
```

```python
import jax
import jax.numpy as jnp
from jax import lax
from jax.experimental import pallas as pl
from jax.experimental.pallas import tpu as pltpu
from jax.sharding import Mesh, PartitionSpec as P

F32 = jnp.float32
BF16 = jnp.bfloat16
LANES = 128
CP = 32
SEQ_HALF = 32
EPS = 1e-05


def dot(a, b, dims):
    return lax.dot_general(a, b, ((dims[:1], dims[1:]), ((), ())), preferred_element_type=F32)


def params(mib):
    return pltpu.CompilerParams(vmem_limit_bytes=mib << 20)


def normalize(x_ref, rows_ref):
    rows = x_ref[...].astype(F32).reshape(256, 256)
    halves = []
    for h in range(2):
        rows_ref[h] = rows[:, h * 128 : h * 128 + 128]
        halves.append(
            jnp.concatenate([rows_ref[h, pl.ds(i, SEQ_HALF, stride=8), :] for i in range(8)], axis=0)
        )
    values = jnp.concatenate(halves, axis=1)
    center = values - jnp.mean(values, axis=1, keepdims=True)
    invstd = lax.rsqrt(jnp.mean(center * center, axis=1, keepdims=True) + EPS)
    return center * invstd, invstd


def project_kernel(x_ref, left_w, right_w, both_ref, normed_ref, rows_ref, block_ref):
    scaled, _ = normalize(x_ref, rows_ref)
    normed = scaled.astype(BF16)
    normed_ref[...] = normed
    left = dot(left_w[...], normed, (1, 1))
    left = jnp.concatenate([left[:, 0:128], left[:, 128:256]], axis=0).astype(BF16)
    right = dot(right_w[...], normed, (1, 1))
    for half in range(2):
        rows_ref[0, 0:32, :] = right[:, half * 128 : half * 128 + 128]
        rows = [rows_ref[0, pl.ds(k, 8, stride=4), :] for k in range(4)]
        for j in range(4):
            block_ref[half * 32 + j * 8 : half * 32 + j * 8 + 8, :] = jnp.concatenate(
                [rows[k][:, j * 32 : j * 32 + 32] for k in range(4)], axis=1
            )
    right = jnp.concatenate(
        [block_ref[pl.ds(h, 8, stride=8), :] for h in range(8)], axis=0
    ).astype(BF16)
    for b in range(8):
        both_ref[b, 0:64] = right
        both_ref[b, 64:128] = left


def route_kernel(own_ref, other_ref, out_ref):
    core, upper, z_own = lax.axis_index("core"), lax.axis_index("col") // 8, lax.axis_index("z")
    left = [own_ref[z_own * 2 + half, 64:128] for half in range(2)]
    none = jnp.zeros((LANES, LANES), BF16)
    for c in range(16):
        out_ref[c, 0:64] = left[0]
        out_ref[c, 64:128] = left[1]
    for z in range(4):
        for owner, rights in ((core, own_ref), (1 - core, other_ref)):
            c = (z * 2 + owner) * 2
            out_ref[c + upper, 128:192] = rights[z * 2, 0:64]
            out_ref[c + upper, 192:256] = rights[z * 2 + 1, 0:64]
            out_ref[c + 1 - upper, 128:256] = none


def fill(blocks, left_ref, gathered, spread):
    odd, seq = lax.axis_index("col") % 2, lax.axis_index("seq")
    lane = lax.broadcasted_iota(jnp.int32, (64, LANES), 1)
    for b in range(8):
        for half in range(2):
            left_ref[b * 64 : b * 64 + 64, half * 128 : half * 128 + 128] = blocks[
                seq * 8 + b, half * 64 : half * 64 + 64
            ]
            gathered[b * 2 + half] = blocks[
                odd * 8 + b, 128 + half * 64 : 192 + half * 64
            ].astype(F32)
    for h in range(8):
        for half in range(2):
            tile = jnp.concatenate(
                [gathered[r * 2 + half, h * 8 : h * 8 + 8, :] for r in range(8)], axis=0
            )
            turned = [tile] + [pltpu.roll(tile, k * 32, 1) for k in range(1, 4)]
            for d in range(4):
                for i in range(4):
                    spread[
                        h, d * 256 + i * 64 : d * 256 + i * 64 + 64, half * 128 : half * 128 + 128
                    ] = jnp.where(lane // 32 == i, turned[(i - d) % 4], 0.0).astype(BF16)


def grads_kernel(
    blocks, cot_hbm, w_scaled_ref, out_ref,
    cot_ref, gathered, spread, left_ref, left_t_ref, grad, left_sum, right_sum, arrived,
):
    copy = pltpu.make_async_copy(cot_hbm, cot_ref, arrived)
    copy.start()
    odd = lax.axis_index("col") % 2
    low = lax.broadcasted_iota(jnp.int32, (32, LANES), 1) < 64
    fill(blocks, left_ref, gathered, spread)
    left_t_ref[...] = left_ref[...].astype(F32).T.astype(BF16)
    copy.wait()
    for i in range(16):
        cot = cot_ref[i * 4 : i * 4 + 4].reshape(256, LANES)
        for h in range(8):
            piece = dot(w_scaled_ref[h * 128 : h * 128 + 128, :], cot, (1, 1)).astype(BF16)
            for d in range(4):
                grad[h, i * 32 : i * 32 + 32, d * 256 : d * 256 + 256] = piece[d * 32 : d * 32 + 32]
    for h in range(8):
        part = dot(grad[h], spread[h], (1, 0))
        left_sum[...] = part if h == 0 else left_sum[...] + part
        for half in range(2):
            parts = []
            part = dot(left_t_ref[half * 128 : half * 128 + 128, :], grad[h], (1, 0))
            for d in range(4):
                lo = part[:, d * 256 : d * 256 + 128]
                hi = part[:, d * 256 + 128 : d * 256 + 256]
                parts.append(
                    jnp.where(low, lo[0:32], lo[32:64]) + jnp.where(low, hi[64:96], hi[96:128])
                )
            turned = jnp.concatenate(parts, axis=0).T
            total = turned[0:64] + turned[64:128]
            for r in range(8):
                right_sum[r * 2 + half, h * 8 : h * 8 + 8, :] = total[r * 8 : r * 8 + 8]
    none = jnp.zeros((LANES, LANES), BF16)
    for b in range(8):
        for half in range(2):
            out_ref[half * 8 + b, 0:64] = left_sum[
                b * 64 : b * 64 + 64, half * 128 : half * 128 + 128
            ].astype(BF16)
            out_ref[odd * 8 + b, 64 + half * 64 : 128 + half * 64] = right_sum[b * 2 + half].astype(BF16)
        out_ref[(1 - odd) * 8 + b, 64:192] = none


def pair_kernel(
    blocks, cot_ref, w_turned_ref, bias_ref, pair_ref, keep_out, send_out,
    gathered, spread, left_ref, outer, wout_sum, wout_rows,
):
    core = lax.axis_index("core")
    fill(blocks, left_ref, gathered, spread)
    left_ref[...] = (left_ref[...].astype(F32) * (1.0 / 64.0)).astype(BF16)
    for h in range(8):
        for d in range(4):
            piece = dot(left_ref[...], spread[h, d * 256 : d * 256 + 256, :], (1, 1)).astype(BF16)
            first = h * 128 + d * 32
            outer[:, first : first + 32, :] = piece.reshape(16, 32, 256)
    for i in range(16):
        cot = cot_ref[i * 4 : i * 4 + 4].reshape(256, LANES)
        tile = outer[i]
        turned = dot(w_turned_ref[...], tile, (1, 0))
        pair_ref[i * 4 : i * 4 + 4] = (
            (turned.T + bias_ref[...]).astype(BF16).reshape(4, 64, LANES)
        )
        part = dot(tile, cot, (1, 0))
        wout_sum[...] = part if i == 0 else wout_sum[...] + part
    for d in range(32):
        wout_rows[pl.ds(d, 32, stride=32), :] = wout_sum[d * 32 : d * 32 + 32, :]
    for z in range(4):
        for half in range(2):
            for out, owner in ((keep_out, core), (send_out, 1 - core)):
                b = (z * 2 + owner) * 2 + half
                out[z * 2 + half] = wout_rows[pl.ds(pl.multiple_of(b * 64, 64), 64), :].astype(BF16)


def sort_kernel(back_ref, keep_w, send_w, left_ref, keep_ref, send_ref):
    core, upper = lax.axis_index("core"), lax.axis_index("col") // 8
    left = back_ref[0, 0:64].astype(F32)
    for b in range(1, 16):
        left += back_ref[b, 0:64].astype(F32)
    left_ref[...] = left.astype(BF16)
    for z in range(4):
        for half in range(2):
            for out, owner, wout in ((keep_ref, core, keep_w), (send_ref, 1 - core, send_w)):
                c = (z * 2 + owner) * 2 + upper
                out[z * 2 + half, 0:64] = back_ref[c, 64 + half * 64 : 128 + half * 64]
                out[z * 2 + half, 64:128] = wout[z * 2 + half]


def turn_grads(left, right, rows_ref, turn_ref):
    rows_ref[...] = right
    rows = [rows_ref[pl.ds(j, 8, stride=8), :] for j in range(8)]
    for half in range(2):
        for k in range(4):
            turn_ref[half, pl.ds(k, 8, stride=4), :] = jnp.concatenate(
                [rows[half * 4 + j][:, k * 32 : k * 32 + 32] for j in range(4)], axis=1
            )
    right = jnp.concatenate([turn_ref[0], turn_ref[1]], axis=1).astype(BF16)
    left = jnp.concatenate([left[0:32], left[32:64]], axis=1).astype(BF16)
    return left, right


def weights_kernel(
    left_ref, right_ref, far_normed, normed_ref, keep_ref, send_ref, rows_ref, turn_ref, total_ref
):
    core = lax.axis_index("core")
    left, right = turn_grads(
        left_ref[...].astype(F32), right_ref[...].astype(F32), rows_ref, turn_ref
    )
    normed = normed_ref[...]
    home = lax.axis_index("col") // 8 == lax.axis_index("seq")
    left_normed = jnp.where(home, normed.astype(F32), far_normed[...].astype(F32)).astype(BF16)
    total = jnp.concatenate(
        [dot(left, left_normed, (1, 0)), dot(right, normed, (1, 0))], axis=0
    )
    total_ref[0] = total[:, 0:128]
    total_ref[1] = total[:, 128:256]
    keep_ref[...] = total_ref[core]
    send_ref[...] = total_ref[1 - core].astype(BF16)


def align_kernel(x_ref, left_w, right_w, left_ref, right_ref, align_ref, rows_ref, block_ref, turn_ref):
    scaled, invstd = normalize(x_ref, rows_ref)
    left, right = turn_grads(
        left_ref[...].astype(F32), right_ref[...].astype(F32), block_ref, turn_ref
    )
    normed_grad = dot(left, left_w[...], (0, 0)) + dot(right, right_w[...], (0, 0))
    mean_grad = jnp.mean(normed_grad, axis=1, keepdims=True)
    mean_cross = jnp.mean(normed_grad * scaled, axis=1, keepdims=True)
    result = invstd * (normed_grad - mean_grad - scaled * mean_cross)
    for h in range(2):
        for i in range(8):
            rows_ref[h, pl.ds(i, SEQ_HALF, stride=8), :] = result[
                i * 32 : i * 32 + 32, h * 128 : h * 128 + 128
            ]
        align_ref[:, h * 128 : h * 128 + 128] = rows_ref[h]


def last_kernel(own_ref, other_ref, wout_ref, left_ref, right_ref):
    core = lax.axis_index("core")
    sums = []
    for blocks in (own_ref, other_ref):
        weight = blocks[0, 0:64].astype(F32)
        for b in range(1, 8):
            weight += blocks[b, 0:64].astype(F32)
        sums.append(weight * (1.0 / 1024.0))
    for half, weight in enumerate(
        (jnp.where(core == 0, sums[0], sums[1]), jnp.where(core == 0, sums[1], sums[0]))
    ):
        left_ref[:, half * 128 : half * 128 + 128] = weight[0:32]
        right_ref[:, half * 128 : half * 128 + 128] = weight[32:64]
    for z in range(4):
        for half in range(2):
            for blocks, owner in ((own_ref, core), (other_ref, 1 - core)):
                start = pl.multiple_of(((z * 2 + owner) * 2 + half) * 64, 64)
                wout_ref[pl.ds(start, 64), :] = blocks[z * 2 + half, 64:128].astype(F32) * (
                    1.0 / 1024.0
                )


def body(alignment, left_weight, right_weight, out_weight, out_bias, cotangent):
    cols_n, seq_n = lax.axis_size("col"), lax.axis_size("seq")
    column = ("z", "seq")
    swap = [
        (c * seq_n + s, c * seq_n + s if c // 8 == s else (c ^ 8) * seq_n + 1 - s)
        for c in range(cols_n)
        for s in range(seq_n)
    ]
    struct = jax.ShapeDtypeStruct
    vmem = pltpu.VMEM
    left_w, right_w = left_weight.T, right_weight.T
    w_rows = out_weight.reshape(CP, CP, LANES).transpose(1, 0, 2).reshape(CP * CP, LANES)
    w_scaled = (w_rows.astype(F32) * (1.0 / 64.0)).astype(BF16)
    w_turned = w_rows.T
    col = lax.axis_index("col")
    seq = lax.axis_index("seq")
    def exchange(value, axes):
        return lax.all_to_all(value, axes, 0, 0, tiled=True)

    def gather(value, axes, count):
        return exchange(jnp.broadcast_to(value, (count,) + value.shape), axes)

    def total(value):
        return jnp.sum(value.astype(F32), axis=0).astype(BF16)

    def other_core(value):
        return lax.ppermute(value, "core", [(0, 1), (1, 0)])

    def cost(flops, nbytes):
        return pl.CostEstimate(flops=flops, bytes_accessed=nbytes, transcendentals=0)

    def in_hbm(value):
        return pltpu.with_memory_space_constraint(value, pltpu.HBM)

    block = struct((64, LANES), BF16)
    both, normed = pl.pallas_call(
        project_kernel,
        out_shape=(struct((8, 128, LANES), BF16), struct((256, 256), BF16)),
        scratch_shapes=[vmem((2, 256, LANES), F32), vmem((64, LANES), F32)],
        compiler_params=params(8),
        name="project",
    )(in_hbm(alignment), in_hbm(left_w), in_hbm(right_w))

    both = exchange(both, column)
    vm, hbm = pl.BlockSpec(memory_space=vmem), pl.BlockSpec(memory_space=pl.ANY)
    blocks = pl.pallas_call(
        route_kernel,
        in_specs=[vm, vm],
        out_shape=struct((16, 256, LANES), BF16),
        compiler_params=params(8),
        name="route",
    )(both, other_core(both))
    blocks = exchange(blocks, "col")
    to_home = [(c * seq_n + 1 - c // 8, c * seq_n + c // 8) for c in range(cols_n)]
    across = [(c * seq_n + c // 8, (c ^ 8) * seq_n + c // 8) for c in range(cols_n)]
    far_normed = lax.ppermute(normed, ("col", "seq"), to_home)
    blocks, far_normed = lax.optimization_barrier((blocks, far_normed))

    gathered, spread = vmem((16, 64, LANES), F32), vmem((8, 1024, 256), BF16)
    left_rows = vmem((512, 256), BF16)
    back = pl.pallas_call(
        grads_kernel,
        in_specs=[vm, hbm, vm],
        out_shape=struct((16, 192, LANES), BF16),
        scratch_shapes=[
            vmem((64, 64, LANES), BF16),
            gathered,
            spread,
            left_rows,
            vmem((256, 512), BF16),
            vmem((8, 512, 1024), BF16),
            vmem((512, 256), F32),
            vmem((16, 64, LANES), F32),
            pltpu.SemaphoreType.DMA,
        ],
        compiler_params=params(24),
        cost_estimate=cost(4 << 30, 4 << 20),
        name="grads",
    )(blocks, in_hbm(cotangent), w_scaled)
    far_normed, back = lax.optimization_barrier((far_normed, back))
    far_normed = lax.ppermute(far_normed, ("col", "seq"), across)
    back, far_normed = lax.optimization_barrier((exchange(back, "col"), far_normed))
    eight = struct((8, 64, LANES), BF16)
    pair, keep, send = pl.pallas_call(
        pair_kernel,
        in_specs=[vm] * 4,
        out_shape=(struct((64, 64, LANES), BF16), eight, eight),
        scratch_shapes=[
            gathered,
            spread,
            left_rows,
            vmem((16, 1024, 256), BF16),
            vmem((1024, LANES), F32),
            vmem((1024, LANES), F32),
        ],
        compiler_params=params(24),
        cost_estimate=cost(4 << 30, 4 << 20),
        name="pair_tile",
    )(blocks, in_hbm(cotangent), w_turned, out_bias.reshape(1, LANES))
    sixteen = struct((8, 128, LANES), BF16)
    left_grad, keep, send = pl.pallas_call(
        sort_kernel,
        in_specs=[vm] * 3,
        out_shape=(block, sixteen, sixteen),
        compiler_params=params(8),
        name="sort",
    )(back, keep, send)
    first = total(exchange((keep.astype(F32) + other_core(send).astype(F32)).astype(BF16), column))
    right_grad = first[:64]
    keep_w, send_w = pl.pallas_call(
        weights_kernel,
        out_shape=(struct((64, LANES), F32), block),
        scratch_shapes=[
            vmem((64, LANES), F32),
            vmem((2, 32, LANES), F32),
            vmem((2, 64, LANES), F32),
        ],
        compiler_params=params(8),
        name="weight_grads",
    )(left_grad, right_grad, far_normed, normed)
    weight = (keep_w + other_core(send_w).astype(F32)).astype(BF16)
    stage = total(gather(jnp.concatenate([weight, first[64:]], axis=0), "col", 16))
    left_grad = lax.ppermute(left_grad, ("col", "seq"), swap)
    stage, left_grad = lax.optimization_barrier((stage, left_grad))
    last = gather(stage, column, 8)
    align_grad = pl.pallas_call(
        align_kernel,
        out_shape=struct((256, 256), F32),
        scratch_shapes=[vmem((2, 256, LANES), F32), vmem((64, LANES), F32), vmem((2, 32, LANES), F32)],
        compiler_params=params(8),
        cost_estimate=cost(1 << 24, 1 << 20),
        name="align",
    )(in_hbm(alignment), left_w, right_w, left_grad, right_grad)
    last, align_grad = lax.optimization_barrier((last, align_grad))
    wout_grad, left_weight_grad, right_weight_grad = pl.pallas_call(
        last_kernel,
        out_shape=(struct((1024, LANES), F32), struct((32, 256), F32), struct((32, 256), F32)),
        compiler_params=params(8),
        name="last",
    )(last, other_core(last))
    return (
        pair,
        align_grad.reshape(alignment.shape),
        left_weight_grad.T,
        right_weight_grad.T,
        wout_grad,
    )


def solution(mesh):
    z = mesh.shape["row"] // 2
    fine = Mesh(
        mesh.devices.reshape(z, 2, mesh.shape["col"], mesh.shape["seq"]), ("z", "core", "col", "seq")
    )
    row = ("z", "core")
    tiles, blocks = P(row + ("seq",), "col", None), P("seq", row + ("col",), None)
    return jax.shard_map(
        body,
        mesh=fine,
        in_specs=(blocks, P(), P(), P(), P(), tiles),
        out_specs=(tiles, blocks, P(), P(), P()),
        check_vma=False,
    )
```

```python
import jax
import jax.numpy as jnp
from jax import lax
from jax.experimental import pallas as pl
from jax.experimental.pallas import tpu as pltpu
from jax.sharding import Mesh, PartitionSpec as P

F32 = jnp.float32
BF16 = jnp.bfloat16
LANES = 128
CP = 32
SEQ_HALF = 32
EPS = 1e-05


def dot(a, b, dims):
    return lax.dot_general(a, b, ((dims[:1], dims[1:]), ((), ())), preferred_element_type=F32)


def params(mib):
    return pltpu.CompilerParams(vmem_limit_bytes=mib << 20)


def normalize(x_ref, rows_ref):
    rows = x_ref[...].astype(F32).reshape(256, 256)
    halves = []
    for h in range(2):
        rows_ref[h] = rows[:, h * 128 : h * 128 + 128]
        halves.append(
            jnp.concatenate([rows_ref[h, pl.ds(i, SEQ_HALF, stride=8), :] for i in range(8)], axis=0)
        )
    values = jnp.concatenate(halves, axis=1)
    center = values - jnp.mean(values, axis=1, keepdims=True)
    invstd = lax.rsqrt(jnp.mean(center * center, axis=1, keepdims=True) + EPS)
    return center * invstd, invstd


def project_kernel(x_ref, left_w, right_w, both_ref, normed_ref, rows_ref, block_ref):
    scaled, _ = normalize(x_ref, rows_ref)
    normed = scaled.astype(BF16)
    normed_ref[...] = normed
    left = dot(left_w[...], normed, (1, 1))
    left = jnp.concatenate([left[:, 0:128], left[:, 128:256]], axis=0).astype(BF16)
    right = dot(right_w[...], normed, (1, 1))
    for half in range(2):
        rows_ref[0, 0:32, :] = right[:, half * 128 : half * 128 + 128]
        rows = [rows_ref[0, pl.ds(k, 8, stride=4), :] for k in range(4)]
        for j in range(4):
            block_ref[half * 32 + j * 8 : half * 32 + j * 8 + 8, :] = jnp.concatenate(
                [rows[k][:, j * 32 : j * 32 + 32] for k in range(4)], axis=1
            )
    right = jnp.concatenate(
        [block_ref[pl.ds(h, 8, stride=8), :] for h in range(8)], axis=0
    ).astype(BF16)
    for b in range(8):
        both_ref[b, 0:64] = right
        both_ref[b, 64:128] = left


def route_kernel(own_ref, other_ref, out_ref):
    core, upper, z_own = lax.axis_index("core"), lax.axis_index("col") // 8, lax.axis_index("z")
    left = [own_ref[z_own * 2 + half, 64:128] for half in range(2)]
    none = jnp.zeros((LANES, LANES), BF16)
    for c in range(16):
        out_ref[c, 0:64] = left[0]
        out_ref[c, 64:128] = left[1]
    for z in range(4):
        for owner, rights in ((core, own_ref), (1 - core, other_ref)):
            c = (z * 2 + owner) * 2
            out_ref[c + upper, 128:192] = rights[z * 2, 0:64]
            out_ref[c + upper, 192:256] = rights[z * 2 + 1, 0:64]
            out_ref[c + 1 - upper, 128:256] = none


def fill(blocks, left_ref, gathered, spread):
    odd, seq = lax.axis_index("col") % 2, lax.axis_index("seq")
    lane = lax.broadcasted_iota(jnp.int32, (64, LANES), 1)
    for b in range(8):
        for half in range(2):
            left_ref[b * 64 : b * 64 + 64, half * 128 : half * 128 + 128] = blocks[
                seq * 8 + b, half * 64 : half * 64 + 64
            ]
            gathered[b * 2 + half] = blocks[
                odd * 8 + b, 128 + half * 64 : 192 + half * 64
            ].astype(F32)
    for h in range(8):
        for half in range(2):
            tile = jnp.concatenate(
                [gathered[r * 2 + half, h * 8 : h * 8 + 8, :] for r in range(8)], axis=0
            )
            turned = [tile] + [pltpu.roll(tile, k * 32, 1) for k in range(1, 4)]
            for d in range(4):
                for i in range(4):
                    spread[
                        h, d * 256 + i * 64 : d * 256 + i * 64 + 64, half * 128 : half * 128 + 128
                    ] = jnp.where(lane // 32 == i, turned[(i - d) % 4], 0.0).astype(BF16)


def grads_kernel(
    blocks, cot_hbm, w_scaled_ref, out_ref,
    cot_ref, gathered, spread, left_ref, left_t_ref, grad, left_sum, right_sum, arrived,
):
    copy = pltpu.make_async_copy(cot_hbm, cot_ref, arrived)
    copy.start()
    odd = lax.axis_index("col") % 2
    low = lax.broadcasted_iota(jnp.int32, (32, LANES), 1) < 64
    fill(blocks, left_ref, gathered, spread)
    left_t_ref[...] = left_ref[...].astype(F32).T.astype(BF16)
    copy.wait()
    for i in range(16):
        cot = cot_ref[i * 4 : i * 4 + 4].reshape(256, LANES)
        for h in range(8):
            piece = dot(w_scaled_ref[h * 128 : h * 128 + 128, :], cot, (1, 1)).astype(BF16)
            for d in range(4):
                grad[h, i * 32 : i * 32 + 32, d * 256 : d * 256 + 256] = piece[d * 32 : d * 32 + 32]
    for h in range(8):
        part = dot(grad[h], spread[h], (1, 0))
        left_sum[...] = part if h == 0 else left_sum[...] + part
        for half in range(2):
            parts = []
            part = dot(left_t_ref[half * 128 : half * 128 + 128, :], grad[h], (1, 0))
            for d in range(4):
                lo = part[:, d * 256 : d * 256 + 128]
                hi = part[:, d * 256 + 128 : d * 256 + 256]
                parts.append(
                    jnp.where(low, lo[0:32], lo[32:64]) + jnp.where(low, hi[64:96], hi[96:128])
                )
            turned = jnp.concatenate(parts, axis=0).T
            total = turned[0:64] + turned[64:128]
            for r in range(8):
                right_sum[r * 2 + half, h * 8 : h * 8 + 8, :] = total[r * 8 : r * 8 + 8]
    none = jnp.zeros((LANES, LANES), BF16)
    for b in range(8):
        for half in range(2):
            out_ref[half * 8 + b, 0:64] = left_sum[
                b * 64 : b * 64 + 64, half * 128 : half * 128 + 128
            ].astype(BF16)
            out_ref[odd * 8 + b, 64 + half * 64 : 128 + half * 64] = right_sum[b * 2 + half].astype(BF16)
        out_ref[(1 - odd) * 8 + b, 64:192] = none


def pair_kernel(
    blocks, cot_hbm, w_turned_ref, bias_ref, pair_ref, keep_out, send_out,
    cot_ref, gathered, spread, left_ref, outer, wout_sum, wout_rows, arrived,
):
    copy = pltpu.make_async_copy(cot_hbm, cot_ref, arrived)
    copy.start()
    core = lax.axis_index("core")
    fill(blocks, left_ref, gathered, spread)
    left_ref[...] = (left_ref[...].astype(F32) * (1.0 / 64.0)).astype(BF16)
    for h in range(8):
        for d in range(4):
            piece = dot(left_ref[...], spread[h, d * 256 : d * 256 + 256, :], (1, 1)).astype(BF16)
            first = h * 128 + d * 32
            outer[:, first : first + 32, :] = piece.reshape(16, 32, 256)
    copy.wait()
    for i in range(16):
        cot = cot_ref[i * 4 : i * 4 + 4].reshape(256, LANES)
        tile = outer[i]
        turned = dot(w_turned_ref[...], tile, (1, 0))
        pair_ref[i * 4 : i * 4 + 4] = (
            (turned.T + bias_ref[...]).astype(BF16).reshape(4, 64, LANES)
        )
        part = dot(tile, cot, (1, 0))
        wout_sum[...] = part if i == 0 else wout_sum[...] + part
    for d in range(32):
        wout_rows[pl.ds(d, 32, stride=32), :] = wout_sum[d * 32 : d * 32 + 32, :]
    for z in range(4):
        for half in range(2):
            for out, owner in ((keep_out, core), (send_out, 1 - core)):
                b = (z * 2 + owner) * 2 + half
                out[z * 2 + half] = wout_rows[pl.ds(pl.multiple_of(b * 64, 64), 64), :].astype(BF16)


def sort_kernel(back_ref, keep_w, send_w, left_ref, keep_ref, send_ref):
    core, upper = lax.axis_index("core"), lax.axis_index("col") // 8
    left = back_ref[0, 0:64].astype(F32)
    for b in range(1, 16):
        left += back_ref[b, 0:64].astype(F32)
    left_ref[...] = left.astype(BF16)
    for z in range(4):
        for half in range(2):
            for out, owner, wout in ((keep_ref, core, keep_w), (send_ref, 1 - core, send_w)):
                c = (z * 2 + owner) * 2 + upper
                out[z * 2 + half, 0:64] = back_ref[c, 64 + half * 64 : 128 + half * 64]
                out[z * 2 + half, 64:128] = wout[z * 2 + half]


def turn_grads(left, right, rows_ref, turn_ref):
    rows_ref[...] = right
    rows = [rows_ref[pl.ds(j, 8, stride=8), :] for j in range(8)]
    for half in range(2):
        for k in range(4):
            turn_ref[half, pl.ds(k, 8, stride=4), :] = jnp.concatenate(
                [rows[half * 4 + j][:, k * 32 : k * 32 + 32] for j in range(4)], axis=1
            )
    right = jnp.concatenate([turn_ref[0], turn_ref[1]], axis=1).astype(BF16)
    left = jnp.concatenate([left[0:32], left[32:64]], axis=1).astype(BF16)
    return left, right


def weights_kernel(
    left_ref, right_ref, far_normed, normed_ref, keep_ref, send_ref, rows_ref, turn_ref, total_ref
):
    core = lax.axis_index("core")
    left, right = turn_grads(
        left_ref[...].astype(F32), right_ref[...].astype(F32), rows_ref, turn_ref
    )
    normed = normed_ref[...]
    home = lax.axis_index("col") // 8 == lax.axis_index("seq")
    left_normed = jnp.where(home, normed.astype(F32), far_normed[...].astype(F32)).astype(BF16)
    total = jnp.concatenate(
        [dot(left, left_normed, (1, 0)), dot(right, normed, (1, 0))], axis=0
    )
    total_ref[0] = total[:, 0:128]
    total_ref[1] = total[:, 128:256]
    keep_ref[...] = total_ref[core]
    send_ref[...] = total_ref[1 - core].astype(BF16)


def align_kernel(x_ref, left_w, right_w, left_ref, right_ref, align_ref, rows_ref, block_ref, turn_ref):
    scaled, invstd = normalize(x_ref, rows_ref)
    left, right = turn_grads(
        left_ref[...].astype(F32), right_ref[...].astype(F32), block_ref, turn_ref
    )
    normed_grad = dot(left, left_w[...], (0, 0)) + dot(right, right_w[...], (0, 0))
    mean_grad = jnp.mean(normed_grad, axis=1, keepdims=True)
    mean_cross = jnp.mean(normed_grad * scaled, axis=1, keepdims=True)
    result = invstd * (normed_grad - mean_grad - scaled * mean_cross)
    for h in range(2):
        for i in range(8):
            rows_ref[h, pl.ds(i, SEQ_HALF, stride=8), :] = result[
                i * 32 : i * 32 + 32, h * 128 : h * 128 + 128
            ]
        align_ref[:, h * 128 : h * 128 + 128] = rows_ref[h]


def last_kernel(own_ref, other_ref, wout_ref, left_ref, right_ref):
    core = lax.axis_index("core")
    sums = []
    for blocks in (own_ref, other_ref):
        weight = blocks[0, 0:64].astype(F32)
        for b in range(1, 8):
            weight += blocks[b, 0:64].astype(F32)
        sums.append(weight * (1.0 / 1024.0))
    for half, weight in enumerate(
        (jnp.where(core == 0, sums[0], sums[1]), jnp.where(core == 0, sums[1], sums[0]))
    ):
        left_ref[:, half * 128 : half * 128 + 128] = weight[0:32]
        right_ref[:, half * 128 : half * 128 + 128] = weight[32:64]
    for z in range(4):
        for half in range(2):
            for blocks, owner in ((own_ref, core), (other_ref, 1 - core)):
                start = pl.multiple_of(((z * 2 + owner) * 2 + half) * 64, 64)
                wout_ref[pl.ds(start, 64), :] = blocks[z * 2 + half, 64:128].astype(F32) * (
                    1.0 / 1024.0
                )


def body(alignment, left_weight, right_weight, out_weight, out_bias, cotangent):
    cols_n, seq_n = lax.axis_size("col"), lax.axis_size("seq")
    column = ("z", "seq")
    swap = [
        (c * seq_n + s, c * seq_n + s if c // 8 == s else (c ^ 8) * seq_n + 1 - s)
        for c in range(cols_n)
        for s in range(seq_n)
    ]
    struct = jax.ShapeDtypeStruct
    vmem = pltpu.VMEM
    left_w, right_w = left_weight.T, right_weight.T
    w_rows = out_weight.reshape(CP, CP, LANES).transpose(1, 0, 2).reshape(CP * CP, LANES)
    w_scaled = (w_rows.astype(F32) * (1.0 / 64.0)).astype(BF16)
    w_turned = w_rows.T
    col = lax.axis_index("col")
    seq = lax.axis_index("seq")
    def exchange(value, axes):
        return lax.all_to_all(value, axes, 0, 0, tiled=True)

    def gather(value, axes, count):
        return exchange(jnp.broadcast_to(value, (count,) + value.shape), axes)

    def total(value):
        return jnp.sum(value.astype(F32), axis=0).astype(BF16)

    def other_core(value):
        return lax.ppermute(value, "core", [(0, 1), (1, 0)])

    def cost(flops, nbytes):
        return pl.CostEstimate(flops=flops, bytes_accessed=nbytes, transcendentals=0)

    def in_hbm(value):
        return pltpu.with_memory_space_constraint(value, pltpu.HBM)

    block = struct((64, LANES), BF16)
    both, normed = pl.pallas_call(
        project_kernel,
        out_shape=(struct((8, 128, LANES), BF16), struct((256, 256), BF16)),
        scratch_shapes=[vmem((2, 256, LANES), F32), vmem((64, LANES), F32)],
        compiler_params=params(8),
        name="project",
    )(in_hbm(alignment), in_hbm(left_w), in_hbm(right_w))

    both = exchange(both, column)
    vm, hbm = pl.BlockSpec(memory_space=vmem), pl.BlockSpec(memory_space=pl.ANY)
    blocks = pl.pallas_call(
        route_kernel,
        in_specs=[vm, vm],
        out_shape=struct((16, 256, LANES), BF16),
        compiler_params=params(8),
        name="route",
    )(both, other_core(both))
    blocks = exchange(blocks, "col")
    to_home = [(c * seq_n + 1 - c // 8, c * seq_n + c // 8) for c in range(cols_n)]
    across = [(c * seq_n + c // 8, (c ^ 8) * seq_n + c // 8) for c in range(cols_n)]
    far_normed = lax.ppermute(normed, ("col", "seq"), to_home)
    blocks, far_normed = lax.optimization_barrier((blocks, far_normed))

    gathered, spread = vmem((16, 64, LANES), F32), vmem((8, 1024, 256), BF16)
    left_rows = vmem((512, 256), BF16)
    back = pl.pallas_call(
        grads_kernel,
        in_specs=[vm, hbm, vm],
        out_shape=struct((16, 192, LANES), BF16),
        scratch_shapes=[
            vmem((64, 64, LANES), BF16),
            gathered,
            spread,
            left_rows,
            vmem((256, 512), BF16),
            vmem((8, 512, 1024), BF16),
            vmem((512, 256), F32),
            vmem((16, 64, LANES), F32),
            pltpu.SemaphoreType.DMA,
        ],
        compiler_params=params(24),
        cost_estimate=cost(4 << 30, 4 << 20),
        name="grads",
    )(blocks, in_hbm(cotangent), w_scaled)
    far_normed, back = lax.optimization_barrier((far_normed, back))
    far_normed = lax.ppermute(far_normed, ("col", "seq"), across)
    back, far_normed = lax.optimization_barrier((exchange(back, "col"), far_normed))
    eight = struct((8, 64, LANES), BF16)
    pair, keep, send = pl.pallas_call(
        pair_kernel,
        in_specs=[vm, hbm, vm, vm],
        out_shape=(struct((64, 64, LANES), BF16), eight, eight),
        scratch_shapes=[
            vmem((64, 64, LANES), BF16),
            gathered,
            spread,
            left_rows,
            vmem((16, 1024, 256), BF16),
            vmem((1024, LANES), F32),
            vmem((1024, LANES), F32),
            pltpu.SemaphoreType.DMA,
        ],
        compiler_params=params(24),
        cost_estimate=cost(4 << 30, 4 << 20),
        name="pair_tile",
    )(blocks, in_hbm(cotangent), w_turned, out_bias.reshape(1, LANES))
    sixteen = struct((8, 128, LANES), BF16)
    left_grad, keep, send = pl.pallas_call(
        sort_kernel,
        in_specs=[vm] * 3,
        out_shape=(block, sixteen, sixteen),
        compiler_params=params(8),
        name="sort",
    )(back, keep, send)
    first = total(exchange((keep.astype(F32) + other_core(send).astype(F32)).astype(BF16), column))
    right_grad = first[:64]
    keep_w, send_w = pl.pallas_call(
        weights_kernel,
        out_shape=(struct((64, LANES), F32), block),
        scratch_shapes=[
            vmem((64, LANES), F32),
            vmem((2, 32, LANES), F32),
            vmem((2, 64, LANES), F32),
        ],
        compiler_params=params(8),
        name="weight_grads",
    )(left_grad, right_grad, far_normed, normed)
    weight = (keep_w + other_core(send_w).astype(F32)).astype(BF16)
    stage = total(gather(jnp.concatenate([weight, first[64:]], axis=0), "col", 16))
    left_grad = lax.ppermute(left_grad, ("col", "seq"), swap)
    stage, left_grad = lax.optimization_barrier((stage, left_grad))
    last = gather(stage, column, 8)
    align_grad = pl.pallas_call(
        align_kernel,
        out_shape=struct((256, 256), F32),
        scratch_shapes=[vmem((2, 256, LANES), F32), vmem((64, LANES), F32), vmem((2, 32, LANES), F32)],
        compiler_params=params(8),
        cost_estimate=cost(1 << 24, 1 << 20),
        name="align",
    )(in_hbm(alignment), left_w, right_w, left_grad, right_grad)
    last, align_grad = lax.optimization_barrier((last, align_grad))
    wout_grad, left_weight_grad, right_weight_grad = pl.pallas_call(
        last_kernel,
        out_shape=(struct((1024, LANES), F32), struct((32, 256), F32), struct((32, 256), F32)),
        compiler_params=params(8),
        name="last",
    )(last, other_core(last))
    return (
        pair,
        align_grad.reshape(alignment.shape),
        left_weight_grad.T,
        right_weight_grad.T,
        wout_grad,
    )


def solution(mesh):
    z = mesh.shape["row"] // 2
    fine = Mesh(
        mesh.devices.reshape(z, 2, mesh.shape["col"], mesh.shape["seq"]), ("z", "core", "col", "seq")
    )
    row = ("z", "core")
    tiles, blocks = P(row + ("seq",), "col", None), P("seq", row + ("col",), None)
    return jax.shard_map(
        body,
        mesh=fine,
        in_specs=(blocks, P(), P(), P(), P(), tiles),
        out_specs=(tiles, blocks, P(), P(), P()),
        check_vma=False,
    )
```
